32 devices in a mesh: freq: 8 (over z, x), row: 4 (over y, core).
Axes of the slice: x: 2, y: 2, z: 4, core: 2. Of those that a mesh axis runs over, the one named last changes fastest.
Arguments:
- operator: bfloat16 [8, 1024, 2, 1024], P('freq', 'row'), may hold values from -0.125 to 0.125
- recorded: bfloat16 [8, 1024, 2, 512], P('freq', 'row'), may hold values from -6 to 6
- filter_coefficients: float32 [3, 8, 1024], P(None, None, ('row', 'freq')), may hold values from -1.2 to 1.2
- tap_delays: int32 [8], replicated, may hold values from 0 to 63, as said below
Outputs:
- primaries: bfloat16 [1024, 512, 1024], P(('row', 'freq'))
The draws below stay inside these ranges and needn't reach their ends.
Inputs may be any that keep to these rules, and one draw needn't show every extreme that they name: `tap_delays`: the delays are not distinct in general; at least one tap has delay 64 - 1.
All inputs are finite; a program needn't handle non-finite values.
Results may differ from the reference program's by a relative error of at most 0.008.
Values may be sent and summed in bfloat16 or wider, within the bound.
A program may use at most 192 MiB of HBM per device.

```python
import math
import jax
import jax.numpy as jnp
from jax import lax

NS = 1024
NC = 512
NT = 1024
TAPS = 8
MAXLAG = 64
NF = 8
N_ROW = 4


def draw_tap_delays(key, part):
    first_key, second_key = jax.random.split(jax.random.fold_in(key, 17))
    values = jax.random.randint(first_key, (TAPS,), 0, MAXLAG)
    position = jax.random.randint(second_key, (), 0, TAPS)
    return values.at[position].set(MAXLAG - 1).astype(jnp.int32)


def levels(key, extent, cuts, least, top_value):
    loudness, own = 1.0, jax.random.fold_in(key, 6)
    for dim, shards_of in cuts:
        draws = jnp.exp(jax.random.uniform(jax.random.fold_in(own, dim), (shards_of,), jnp.float32, least / len(cuts), top_value / len(cuts)))
        loudness = loudness * jnp.repeat(draws, extent[dim] // shards_of).reshape([-1 if axis == dim else 1 for axis in range(len(extent))])
    return loudness


def bell_draw(stream_key, shape, width, bound, pieces=(), held_as=jnp.bfloat16):
    array = width * jax.random.normal(stream_key, shape, jnp.float32)
    if pieces:
        array = array * levels(stream_key, shape, pieces, -0.22, 0.18)
    return jnp.clip(array, -bound, bound).astype(held_as)


def setup_inputs(seed: int = 0) -> dict:
    seeds = jax.random.split(jax.random.key(seed), 5)
    return {
        "operator": bell_draw(seeds[0], (NF, NS, 2, NS), (2 * NS) ** -0.5, 0.125, ((0, 8), (1, 4))),
        "recorded": bell_draw(seeds[1], (NF, NS, 2, NC), 1.0, 6.0, ((0, 8), (1, 4))),
        "filter_coefficients": bell_draw(seeds[2], (3, TAPS, NS), 0.2, 1.2, ((2, 32),), jnp.float32),
        "tap_delays": draw_tap_delays(jax.random.fold_in(seeds[4], 71), 0),
    }


shrink_level = 0.5

def inverse_lookup(harmonics, time_step_total):
    overtone_indices = (jnp.arange(harmonics) + 1).astype(jnp.int32)
    recording_epochs = jnp.arange(time_step_total).astype(jnp.int32)
    rotation_radians = (overtone_indices[:, None] * recording_epochs[None, :] % time_step_total).astype(jnp.float32) * (2.0 * math.pi / time_step_total)
    scale = 1.0 / math.sqrt(harmonics)
    return jnp.stack([jnp.cos(rotation_radians) * scale, -jnp.sin(rotation_radians) * scale], axis=1).astype(jnp.bfloat16)

def complex_block(columns, segment):
    real_component = segment[:, 0]
    imag_part = segment[:, 1]
    upper = jnp.concatenate([real_component, imag_part], axis=1)
    lower = jnp.concatenate([-imag_part, real_component], axis=1)
    return jnp.dot(columns, jnp.concatenate([upper, lower], axis=0), preferred_element_type=jnp.float32)

def match_filter(border_rows, weights, tap_delays, row_count, time_step_total):
    padded = jnp.pad(border_rows, ((0, 0), (0, 0), (MAXLAG, 0)))
    estimate = jnp.zeros((row_count, border_rows.shape[1], time_step_total), jnp.float32)
    anchor = jnp.zeros((), jnp.int32)
    for tap_index in range(weights.shape[1]):
        begin = (MAXLAG - tap_delays[tap_index]).astype(jnp.int32)
        displaced_trace = lax.dynamic_slice(padded, (anchor, anchor, begin), (padded.shape[0], padded.shape[1], time_step_total))
        for neighbour in range(3):
            factor = weights[neighbour, tap_index][:, None, None]
            estimate = estimate + factor * displaced_trace[neighbour:neighbour + row_count].astype(jnp.float32)
    return estimate

def shrink(data_time, estimate):
    residual = data_time.astype(jnp.float32) - estimate
    return (jnp.sign(residual) * jnp.maximum(jnp.abs(residual) - shrink_level, 0.0)).astype(jnp.bfloat16)

def reference(operator, recorded, filter_coefficients, tap_delays):

    def one_frequency(pair):
        matrix, multiplicand = pair
        columns = matrix.reshape(NS, 2 * NS)
        return complex_block(columns, multiplicand).astype(jnp.bfloat16).reshape(NS, 2, NC)
    predicted = lax.map(one_frequency, (operator, recorded))
    table = inverse_lookup(NF, NT).astype(jnp.float32)
    line_rows = NS // N_ROW
    predicted_lines = jnp.moveaxis(predicted.reshape(NF, N_ROW, line_rows, 2, NC), 1, 0)
    recorded_lines = jnp.moveaxis(recorded.reshape(NF, N_ROW, line_rows, 2, NC), 1, 0)
    weight_lines = jnp.moveaxis(filter_coefficients.reshape(3, TAPS, N_ROW, line_rows), 2, 0)

    def one_line(triple):
        predicted_part, recorded_part, weight_part = triple
        multiples = jnp.einsum('frcs,fct->rst', predicted_part.astype(jnp.float32), table, precision=lax.Precision.HIGHEST).astype(jnp.bfloat16)
        data_time = jnp.einsum('frcs,fct->rst', recorded_part.astype(jnp.float32), table, precision=lax.Precision.HIGHEST).astype(jnp.bfloat16)
        border_rows = jnp.pad(multiples, ((1, 1), (0, 0), (0, 0)))
        estimate = match_filter(border_rows, weight_part, tap_delays, line_rows, NT)
        return shrink(data_time, estimate)
    primaries = lax.map(one_line, (predicted_lines, recorded_lines, weight_lines))
    return primaries.reshape(NS, NC, NT)
```

```python
import functools
import math

import jax
import jax.numpy as jnp
from jax import lax
from jax.experimental import pallas as pl
from jax.experimental.pallas import tpu as pltpu
from jax.sharding import PartitionSpec as P

NT = 1024

shrink_level = 0.5


def inverse_lookup(harmonics, time_step_total):
    overtone_indices = jnp.arange(harmonics) + 1
    recording_epochs = jnp.arange(time_step_total)
    rotation_radians = (
        overtone_indices[:, None] * recording_epochs[None, :] % time_step_total
    ).astype(jnp.float32) * (2.0 * math.pi / time_step_total)
    scale = 1.0 / math.sqrt(harmonics)
    return jnp.stack(
        [jnp.cos(rotation_radians) * scale, -jnp.sin(rotation_radians) * scale], axis=1
    ).astype(jnp.bfloat16)


def time_kernel(
    per_step, weights_ref, delays_ref, table_ref, recorded_ref, predicted_ref, out_ref, shifted, basis
):
    taps, depth, times = shifted.shape
    step = pl.program_id(0)
    part = min(depth, 16)

    @pl.when(step == 0)
    def _():
        @pl.loop(0, depth // part)
        def _(block):
            at = pl.ds(pl.multiple_of(block * part, part), part)
            table = table_ref[at, :].astype(jnp.float32)
            position = lax.broadcasted_iota(jnp.int32, table.shape, 1)
            for tap in range(taps):
                delay = delays_ref[tap]
                moved = pltpu.roll(table, delay, 1)
                shifted[tap, at, :] = jnp.where(position >= delay, moved, 0.0)
            for slot in range(per_step):
                basis[slot, at, :] = table_ref[at, :]

    for slot in range(per_step):
        station = step * per_step + slot

        @pl.loop(0, depth // part)
        def _(block):
            at = pl.multiple_of(block * part, part)
            for column in range(0, times, 512):
                columns = pl.ds(column, 512)
                moved = [shifted[tap, pl.ds(at, part), columns] for tap in range(taps)]
                for neighbour in range(3):
                    total = moved[0] * -weights_ref[neighbour, 0, station]
                    for tap in range(1, taps):
                        total = total - moved[tap] * weights_ref[neighbour, tap, station]
                    rows = pl.ds(pl.multiple_of((neighbour + 1) * depth + at, part), part)
                    basis[slot, rows, columns] = total.astype(jnp.bfloat16)

        spectra = jnp.concatenate(
            [recorded_ref[station]] + [predicted_ref[station + n] for n in range(3)], axis=0
        )
        for column in range(0, times, 256):
            residual = lax.dot_general(
                spectra,
                basis[slot, :, column : column + 256],
                (((0,), (0,)), ((), ())),
                preferred_element_type=jnp.float32,
            )
            clipped = jnp.clip(residual, -shrink_level, shrink_level)
            out_ref[slot, :, column : column + 256] = (residual - clipped).astype(jnp.bfloat16)


def to_primaries(weights, delays, table, recorded, predicted):
    rows, depth, columns = recorded.shape
    taps, times = weights.shape[1], table.shape[1]
    per_step = 2 if rows % 2 == 0 else 1
    return pl.pallas_call(
        functools.partial(time_kernel, per_step),
        grid=(rows // per_step,),
        out_shape=jax.ShapeDtypeStruct((rows, columns, times), jnp.bfloat16),
        in_specs=[
            pl.BlockSpec(memory_space=pltpu.SMEM),
            pl.BlockSpec(memory_space=pltpu.SMEM),
            pl.BlockSpec(memory_space=pltpu.VMEM),
            pl.BlockSpec(memory_space=pltpu.VMEM),
            pl.BlockSpec(memory_space=pltpu.VMEM),
        ],
        out_specs=pl.BlockSpec((per_step, columns, times), lambda i: (i, 0, 0)),
        scratch_shapes=[
            pltpu.VMEM((taps, depth, times), jnp.float32),
            pltpu.VMEM((per_step, 4 * depth, times), jnp.bfloat16),
        ],
        compiler_params=pltpu.CompilerParams(vmem_limit_bytes=40 * 1024 * 1024),
        cost_estimate=pl.CostEstimate(
            flops=8 * rows * columns * depth * times,
            bytes_accessed=2 * rows * columns * times,
            transcendentals=0,
        ),
    )(weights, delays, table, recorded, predicted)


def body(operator, recorded, filter_coefficients, tap_delays):
    stations = operator.shape[1]
    tiles = lax.axis_size("freq")
    rows = stations // tiles
    shots = recorded.shape[3]
    recorded_tiles = lax.all_to_all(
        recorded[0].reshape(tiles, rows, 2, shots), "freq", split_axis=0, concat_axis=0, tiled=True
    )
    segment = lax.all_gather(recorded[0], "row", axis=0, tiled=True)
    segment = segment.reshape(segment.shape[0], 2 * shots)
    with_real = jnp.dot(operator[0, :, 0], segment, preferred_element_type=jnp.float32)
    with_imag = jnp.dot(operator[0, :, 1], segment, preferred_element_type=jnp.float32)
    predicted = jnp.stack(
        [
            with_real[:, :shots] - with_imag[:, shots:],
            with_real[:, shots:] + with_imag[:, :shots],
        ],
        axis=1,
    ).astype(jnp.bfloat16)
    inner = predicted.reshape(tiles, rows, 2, shots)
    nothing = jnp.zeros((1, 1, 2, shots), jnp.bfloat16)
    before = jnp.concatenate([nothing, inner[:-1, -1:]], axis=0)
    after = jnp.concatenate([inner[1:, :1], nothing], axis=0)
    predicted_tiles = lax.all_to_all(
        jnp.concatenate([before, inner, after], axis=1),
        "freq",
        split_axis=0,
        concat_axis=0,
        tiled=True,
    )
    table = inverse_lookup(tiles, NT).reshape(2 * tiles, NT)

    def by_station(spectra):
        return jnp.swapaxes(spectra, 0, 1).reshape(spectra.shape[1], 2 * tiles, shots)

    return to_primaries(
        filter_coefficients,
        tap_delays,
        table,
        by_station(recorded_tiles),
        by_station(predicted_tiles),
    )


def solution(mesh):
    in_specs = (
        P("freq", "row", None, None),
        P("freq", "row", None, None),
        P(None, None, ("row", "freq")),
        P(),
    )
    out_specs = P(("row", "freq"), None, None)
    return jax.shard_map(body, mesh=mesh, in_specs=in_specs, out_specs=out_specs, check_vma=False)
```

```python
import functools
import math

import jax
import jax.numpy as jnp
from jax import lax
from jax.experimental import pallas as pl
from jax.experimental.pallas import tpu as pltpu
from jax.sharding import PartitionSpec as P

NT = 1024
MESH = pl.DeviceIdType.MESH

shrink_level = 0.5


def inverse_lookup(harmonics, time_step_total):
    overtone_indices = jnp.arange(harmonics) + 1
    recording_epochs = jnp.arange(time_step_total)
    rotation_radians = (
        overtone_indices[:, None] * recording_epochs[None, :] % time_step_total
    ).astype(jnp.float32) * (2.0 * math.pi / time_step_total)
    scale = 1.0 / math.sqrt(harmonics)
    return jnp.stack(
        [jnp.cos(rotation_radians) * scale, -jnp.sin(rotation_radians) * scale], axis=1
    ).astype(jnp.bfloat16)


def time_kernel(
    per_step, weights_ref, delays_ref, table_ref, recorded_ref, predicted_ref, out_ref, shifted, basis
):
    taps, depth, times = shifted.shape
    step = pl.program_id(0)
    part = min(depth, 16)

    @pl.when(step == 0)
    def _():
        @pl.loop(0, depth // part)
        def _(block):
            at = pl.ds(pl.multiple_of(block * part, part), part)
            table = table_ref[at, :].astype(jnp.float32)
            position = lax.broadcasted_iota(jnp.int32, table.shape, 1)
            for tap in range(taps):
                delay = delays_ref[tap]
                moved = pltpu.roll(table, delay, 1)
                shifted[tap, at, :] = jnp.where(position >= delay, moved, 0.0)
            for slot in range(per_step):
                basis[slot, at, :] = table_ref[at, :]

    for slot in range(per_step):
        station = step * per_step + slot

        @pl.loop(0, depth // part)
        def _(block):
            at = pl.multiple_of(block * part, part)
            for column in range(0, times, 512):
                columns = pl.ds(column, 512)
                moved = [shifted[tap, pl.ds(at, part), columns] for tap in range(taps)]
                for neighbour in range(3):
                    total = moved[0] * -weights_ref[neighbour, 0, station]
                    for tap in range(1, taps):
                        total = total - moved[tap] * weights_ref[neighbour, tap, station]
                    rows = pl.ds(pl.multiple_of((neighbour + 1) * depth + at, part), part)
                    basis[slot, rows, columns] = total.astype(jnp.bfloat16)

        spectra = jnp.concatenate(
            [recorded_ref[station]] + [predicted_ref[station + n] for n in range(3)], axis=0
        )
        for column in range(0, times, 256):
            residual = lax.dot_general(
                spectra,
                basis[slot, :, column : column + 256],
                (((0,), (0,)), ((), ())),
                preferred_element_type=jnp.float32,
            )
            clipped = jnp.clip(residual, -shrink_level, shrink_level)
            out_ref[slot, :, column : column + 256] = (residual - clipped).astype(jnp.bfloat16)


def to_primaries(weights, delays, table, recorded, predicted):
    rows, depth, columns = recorded.shape
    taps, times = weights.shape[1], table.shape[1]
    per_step = 2 if rows % 2 == 0 else 1
    return pl.pallas_call(
        functools.partial(time_kernel, per_step),
        grid=(rows // per_step,),
        out_shape=jax.ShapeDtypeStruct((rows, columns, times), jnp.bfloat16),
        in_specs=[
            pl.BlockSpec(memory_space=pltpu.SMEM),
            pl.BlockSpec(memory_space=pltpu.SMEM),
            pl.BlockSpec(memory_space=pltpu.VMEM),
            pl.BlockSpec(memory_space=pltpu.VMEM),
            pl.BlockSpec(memory_space=pltpu.VMEM),
        ],
        out_specs=pl.BlockSpec((per_step, columns, times), lambda i: (i, 0, 0)),
        scratch_shapes=[
            pltpu.VMEM((taps, depth, times), jnp.float32),
            pltpu.VMEM((per_step, 4 * depth, times), jnp.bfloat16),
        ],
        compiler_params=pltpu.CompilerParams(vmem_limit_bytes=40 * 1024 * 1024),
        cost_estimate=pl.CostEstimate(
            flops=8 * rows * columns * depth * times,
            bytes_accessed=2 * rows * columns * times,
            transcendentals=0,
        ),
    )(weights, delays, table, recorded, predicted)


def exchange_kernel(
    tiles,
    lines,
    real_ref,
    imag_ref,
    shard_ref,
    recorded_ref,
    recorded_out,
    predicted_out,
    halo_out,
    segment,
    product,
    predicted,
    halo,
    recorded_sent,
    recorded_got,
    predicted_sent,
    predicted_got,
    halo_sent,
    halo_got,
    own_sent,
    forward_sent,
    shard_got,
):
    mine = lax.axis_index("freq")
    line = lax.axis_index("row")
    sibling = line + 1 - 2 * (line % 2)
    peers = [(line + 2 * k) % lines for k in range(1, lines // 2)]
    stations, width = shard_ref.shape
    shots = width // 2
    rows = stations // tiles

    barrier = pltpu.get_barrier_semaphore()

    @pl.loop(1, tiles)
    def _(k):
        pl.semaphore_signal(
            barrier, inc=1, device_id={"freq": (mine + k) % tiles}, device_id_type=MESH
        )

    for peer in [sibling] + peers:
        pl.semaphore_signal(barrier, inc=1, device_id={"row": peer}, device_id_type=MESH)
    pl.semaphore_wait(barrier, tiles - 1 + 1 + len(peers))

    def own_copy(slot, peer):
        return pltpu.make_async_remote_copy(
            src_ref=shard_ref,
            dst_ref=segment.at[line],
            send_sem=own_sent.at[slot],
            recv_sem=shard_got.at[line],
            device_id={"row": peer},
            device_id_type=MESH,
        )

    def forward_copy(slot, source):
        return pltpu.make_async_remote_copy(
            src_ref=segment.at[source],
            dst_ref=segment.at[source],
            send_sem=forward_sent.at[slot],
            recv_sem=shard_got.at[source],
            device_id={"row": sibling},
            device_id_type=MESH,
        )

    def tile_copy(source, target, sent, got, tile):
        return pltpu.make_async_remote_copy(
            src_ref=source.at[tile],
            dst_ref=target.at[mine],
            send_sem=sent.at[tile],
            recv_sem=got.at[mine],
            device_id={"freq": tile},
            device_id_type=MESH,
        )

    def tile_arrival(source, target, sent, got, tile):
        return pltpu.make_async_remote_copy(
            src_ref=source.at[tile],
            dst_ref=target.at[tile],
            send_sem=sent.at[tile],
            recv_sem=got.at[tile],
            device_id={"freq": tile},
            device_id_type=MESH,
        )

    for slot, peer in enumerate(peers):
        own_copy(slot, peer).start()
    own_copy(len(peers), sibling).start()

    recorded_set = (recorded_ref, recorded_out, recorded_sent, recorded_got)
    predicted_set = (predicted, predicted_out, predicted_sent, predicted_got)
    halo_set = (halo, halo_out, halo_sent, halo_got)

    @pl.loop(1, tiles)
    def _(k):
        tile_copy(*recorded_set, (mine + k) % tiles).start()

    recorded_out[mine] = recorded_ref[mine]

    def accumulate(source, block, first):
        at = pl.ds(pl.multiple_of(source * stations, stations), stations)
        with_real = jnp.dot(real_ref[:, at], block[...], preferred_element_type=jnp.float32)
        with_imag = jnp.dot(imag_ref[:, at], block[...], preferred_element_type=jnp.float32)
        upper = with_real[:, :shots] - with_imag[:, shots:]
        lower = with_real[:, shots:] + with_imag[:, :shots]
        if not first:
            upper = upper + product[:, :shots]
            lower = lower + product[:, shots:]
        product[:, :shots] = upper
        product[:, shots:] = lower

    accumulate(line, shard_ref, True)
    forward_copy(0, sibling).wait_recv()
    accumulate(sibling, segment.at[sibling], False)
    for slot, peer in enumerate(peers):
        forward_copy(slot, peer).wait_recv()
        forward_copy(slot, peer).start()
        accumulate(peer, segment.at[peer], False)
    for slot, peer in enumerate(peers):
        other = peer + 1 - 2 * (peer % 2)
        forward_copy(slot, other).wait_recv()
        accumulate(other, segment.at[other], False)

    @pl.loop(1, tiles + 1)
    def _(k):
        tile = (mine + k) % tiles
        if rows % 16 == 0:
            start = pl.multiple_of(tile * rows, 16)
            inner = product[pl.ds(start, rows), :]
        else:
            inner = jnp.concatenate(
                [product[pl.ds(tile * rows + i, 1), :] for i in range(rows)], axis=0
            )
        predicted[tile] = inner.astype(jnp.bfloat16)
        low = product[pl.ds(jnp.maximum(tile * rows - 1, 0), 1), :]
        high = product[pl.ds(jnp.minimum(tile * rows + rows, stations - 1), 1), :]
        low = jnp.where(tile == 0, 0.0, low)
        high = jnp.where(tile == tiles - 1, 0.0, high)
        pieces = [edge[:, i : i + 128] for edge in (low, high) for i in range(0, width, 128)]
        halo[tile] = jnp.concatenate(pieces, axis=0).astype(jnp.bfloat16)

        @pl.when(k < tiles)
        def _():
            tile_copy(*predicted_set, tile).start()
            tile_copy(*halo_set, tile).start()

    predicted_out[mine] = predicted[mine]
    halo_out[mine] = halo[mine]

    @pl.loop(1, tiles)
    def _(k):
        for transfers in (recorded_set, predicted_set, halo_set):
            tile_arrival(*transfers, (mine + k) % tiles).wait_recv()

    @pl.loop(1, tiles)
    def _(k):
        for transfers in (recorded_set, predicted_set, halo_set):
            tile_copy(*transfers, (mine + k) % tiles).wait_send()

    for slot, peer in enumerate(peers):
        own_copy(slot, peer).wait_send()
        forward_copy(slot, peer).wait_send()
    own_copy(len(peers), sibling).wait_send()


def exchange(real, imag, shard, tiles, lines):
    stations, width = shard.shape
    rows = stations // tiles
    vmem = pl.BlockSpec(memory_space=pltpu.VMEM)
    tile_shape = (tiles, rows, width)
    halo_shape = (tiles, 2 * width // 128, 128)
    sems = pltpu.SemaphoreType.DMA((tiles,))
    return pl.pallas_call(
        functools.partial(exchange_kernel, tiles, lines),
        out_shape=[
            jax.ShapeDtypeStruct(tile_shape, jnp.bfloat16),
            jax.ShapeDtypeStruct(tile_shape, jnp.bfloat16),
            jax.ShapeDtypeStruct(halo_shape, jnp.bfloat16),
        ],
        in_specs=[vmem] * 4,
        out_specs=[vmem] * 3,
        scratch_shapes=[
            pltpu.VMEM((lines, stations, width), jnp.bfloat16),
            pltpu.VMEM((stations, width), jnp.float32),
            pltpu.VMEM(tile_shape, jnp.bfloat16),
            pltpu.VMEM(halo_shape, jnp.bfloat16),
        ]
        + [sems] * 6
        + [pltpu.SemaphoreType.DMA((lines,))] * 3,
        compiler_params=pltpu.CompilerParams(
            collective_id=0, has_side_effects=True, vmem_limit_bytes=40 * 1024 * 1024
        ),
        cost_estimate=pl.CostEstimate(
            flops=8 * lines * stations * stations * width // 2,
            bytes_accessed=2 * (lines + 5) * stations * width,
            transcendentals=0,
        ),
    )(real, imag, shard, shard.reshape(tile_shape))


def body(operator, recorded, filter_coefficients, tap_delays):
    stations = operator.shape[1]
    tiles, lines = lax.axis_size("freq"), lax.axis_size("row")
    rows = stations // tiles
    shots = recorded.shape[3]
    recorded_tiles, predicted_tiles, halo = exchange(
        operator[0, :, 0],
        operator[0, :, 1],
        recorded[0].reshape(stations, 2 * shots),
        tiles,
        lines,
    )
    halo = halo.reshape(tiles, 2, 2 * shots)
    table = inverse_lookup(tiles, NT).reshape(2 * tiles, NT)

    def by_station(spectra):
        return jnp.swapaxes(spectra, 0, 1).reshape(spectra.shape[1], 2 * tiles, shots)

    return to_primaries(
        filter_coefficients,
        tap_delays,
        table,
        by_station(recorded_tiles),
        by_station(jnp.concatenate([halo[:, :1], predicted_tiles, halo[:, 1:]], axis=1)),
    )


def solution(mesh):
    in_specs = (
        P("freq", "row", None, None),
        P("freq", "row", None, None),
        P(None, None, ("row", "freq")),
        P(),
    )
    out_specs = P(("row", "freq"), None, None)
    return jax.shard_map(body, mesh=mesh, in_specs=in_specs, out_specs=out_specs, check_vma=False)
```

```python
import functools
import math

import jax
import jax.numpy as jnp
from jax import lax
from jax.experimental import pallas as pl
from jax.experimental.pallas import tpu as pltpu
from jax.sharding import PartitionSpec as P

NT = 1024
MESH = pl.DeviceIdType.MESH

shrink_level = 0.5


def inverse_lookup(harmonics, time_step_total):
    overtone_indices = jnp.arange(harmonics) + 1
    recording_epochs = jnp.arange(time_step_total)
    rotation_radians = (
        overtone_indices[:, None] * recording_epochs[None, :] % time_step_total
    ).astype(jnp.float32) * (2.0 * math.pi / time_step_total)
    scale = 1.0 / math.sqrt(harmonics)
    return jnp.stack(
        [jnp.cos(rotation_radians) * scale, -jnp.sin(rotation_radians) * scale], axis=1
    ).astype(jnp.bfloat16)


def delay_kernel(delays_ref, table_ref, shifted_ref):
    taps, depth, times = shifted_ref.shape
    part = min(depth, 16)

    @pl.loop(0, depth // part)
    def _(block):
        at = pl.ds(pl.multiple_of(block * part, part), part)
        table = table_ref[at, :].astype(jnp.float32)
        position = lax.broadcasted_iota(jnp.int32, table.shape, 1)
        for tap in range(taps):
            delay = delays_ref[tap]
            moved = pltpu.roll(table, delay, 1)
            shifted_ref[tap, at, :] = jnp.where(position >= delay, moved, 0.0)


def delayed_tables(delays, table):
    vmem = pl.BlockSpec(memory_space=pltpu.VMEM)
    return pl.pallas_call(
        delay_kernel,
        out_shape=jax.ShapeDtypeStruct(delays.shape + table.shape, jnp.float32),
        in_specs=[pl.BlockSpec(memory_space=pltpu.SMEM), vmem],
        out_specs=vmem,
        compiler_params=pltpu.CompilerParams(vmem_limit_bytes=24 * 1024 * 1024),
    )(delays, table)


def filtered_tables(weights_ref, shifted_ref, basis_ref):
    taps, depth, times = shifted_ref.shape
    part = min(depth, 16)

    @pl.loop(0, basis_ref.shape[0])
    def _(station):
        @pl.loop(0, depth // part)
        def _(block):
            at = pl.multiple_of(block * part, part)
            for column in range(0, times, 512):
                columns = pl.ds(column, 512)
                moved = [shifted_ref[tap, pl.ds(at, part), columns] for tap in range(taps)]
                for neighbour in range(3):
                    total = moved[0] * -weights_ref[neighbour, 0, station]
                    for tap in range(1, taps):
                        total = total - moved[tap] * weights_ref[neighbour, tap, station]
                    rows = pl.ds(pl.multiple_of(neighbour * depth + at, part), part)
                    basis_ref[station, rows, columns] = total.astype(jnp.bfloat16)


def time_kernel(per_step, table_ref, basis_ref, recorded_ref, predicted_ref, out_ref):
    step = pl.program_id(0)
    times = table_ref.shape[1]
    for slot in range(per_step):
        station = step * per_step + slot
        spectra = jnp.concatenate(
            [recorded_ref[station]] + [predicted_ref[station + n] for n in range(3)], axis=0
        )
        for column in range(0, times, 256):
            columns = slice(column, column + 256)
            residual = lax.dot_general(
                spectra,
                jnp.concatenate([table_ref[:, columns], basis_ref[slot, :, columns]], axis=0),
                (((0,), (0,)), ((), ())),
                preferred_element_type=jnp.float32,
            )
            clipped = jnp.clip(residual, -shrink_level, shrink_level)
            out_ref[slot, :, columns] = (residual - clipped).astype(jnp.bfloat16)


def to_primaries(table, basis, recorded, predicted):
    rows, depth, columns = recorded.shape
    times = table.shape[1]
    per_step = 2 if rows % 2 == 0 else 1
    vmem = pl.BlockSpec(memory_space=pltpu.VMEM)
    return pl.pallas_call(
        functools.partial(time_kernel, per_step),
        grid=(rows // per_step,),
        out_shape=jax.ShapeDtypeStruct((rows, columns, times), jnp.bfloat16),
        in_specs=[
            vmem,
            pl.BlockSpec((per_step, 3 * depth, times), lambda i: (i, 0, 0)),
            vmem,
            vmem,
        ],
        out_specs=pl.BlockSpec((per_step, columns, times), lambda i: (i, 0, 0)),
        compiler_params=pltpu.CompilerParams(vmem_limit_bytes=40 * 1024 * 1024),
        cost_estimate=pl.CostEstimate(
            flops=8 * rows * columns * depth * times,
            bytes_accessed=2 * rows * columns * times,
            transcendentals=0,
        ),
    )(table, basis, recorded, predicted)


def exchange_kernel(
    tiles,
    lines,
    weights_ref,
    shifted_ref,
    real_ref,
    imag_ref,
    shard_ref,
    recorded_ref,
    recorded_out,
    predicted_out,
    halo_out,
    basis_out,
    segment,
    product,
    predicted,
    halo,
    recorded_sent,
    recorded_got,
    predicted_sent,
    predicted_got,
    halo_sent,
    halo_got,
    own_sent,
    forward_sent,
    shard_got,
):
    mine = lax.axis_index("freq")
    line = lax.axis_index("row")
    sibling = line + 1 - 2 * (line % 2)
    peers = [(line + 2 * k) % lines for k in range(1, lines // 2)]
    stations, width = shard_ref.shape
    shots = width // 2
    rows = stations // tiles

    barrier = pltpu.get_barrier_semaphore()

    @pl.loop(1, tiles)
    def _(k):
        pl.semaphore_signal(
            barrier, inc=1, device_id={"freq": (mine + k) % tiles}, device_id_type=MESH
        )

    for peer in [sibling] + peers:
        pl.semaphore_signal(barrier, inc=1, device_id={"row": peer}, device_id_type=MESH)
    pl.semaphore_wait(barrier, tiles - 1 + 1 + len(peers))

    def own_copy(slot, peer):
        return pltpu.make_async_remote_copy(
            src_ref=shard_ref,
            dst_ref=segment.at[line],
            send_sem=own_sent.at[slot],
            recv_sem=shard_got.at[line],
            device_id={"row": peer},
            device_id_type=MESH,
        )

    def forward_copy(slot, source):
        return pltpu.make_async_remote_copy(
            src_ref=segment.at[source],
            dst_ref=segment.at[source],
            send_sem=forward_sent.at[slot],
            recv_sem=shard_got.at[source],
            device_id={"row": sibling},
            device_id_type=MESH,
        )

    def tile_copy(source, target, sent, got, tile):
        return pltpu.make_async_remote_copy(
            src_ref=source.at[tile],
            dst_ref=target.at[mine],
            send_sem=sent.at[tile],
            recv_sem=got.at[mine],
            device_id={"freq": tile},
            device_id_type=MESH,
        )

    def tile_arrival(source, target, sent, got, tile):
        return pltpu.make_async_remote_copy(
            src_ref=source.at[tile],
            dst_ref=target.at[tile],
            send_sem=sent.at[tile],
            recv_sem=got.at[tile],
            device_id={"freq": tile},
            device_id_type=MESH,
        )

    for slot, peer in enumerate(peers):
        own_copy(slot, peer).start()
    own_copy(len(peers), sibling).start()

    recorded_set = (recorded_ref, recorded_out, recorded_sent, recorded_got)
    predicted_set = (predicted, predicted_out, predicted_sent, predicted_got)
    halo_set = (halo, halo_out, halo_sent, halo_got)

    @pl.loop(1, tiles)
    def _(k):
        tile_copy(*recorded_set, (mine + k) % tiles).start()

    recorded_out[mine] = recorded_ref[mine]

    def accumulate(source, block, first):
        at = pl.ds(pl.multiple_of(source * stations, stations), stations)
        with_real = jnp.dot(real_ref[:, at], block[...], preferred_element_type=jnp.float32)
        with_imag = jnp.dot(imag_ref[:, at], block[...], preferred_element_type=jnp.float32)
        upper = with_real[:, :shots] - with_imag[:, shots:]
        lower = with_real[:, shots:] + with_imag[:, :shots]
        if not first:
            upper = upper + product[:, :shots]
            lower = lower + product[:, shots:]
        product[:, :shots] = upper
        product[:, shots:] = lower

    accumulate(line, shard_ref, True)
    forward_copy(0, sibling).wait_recv()
    accumulate(sibling, segment.at[sibling], False)
    for slot, peer in enumerate(peers):
        forward_copy(slot, peer).wait_recv()
        forward_copy(slot, peer).start()
        accumulate(peer, segment.at[peer], False)
    for slot, peer in enumerate(peers):
        other = peer + 1 - 2 * (peer % 2)
        forward_copy(slot, other).wait_recv()
        accumulate(other, segment.at[other], False)

    @pl.loop(1, tiles + 1)
    def _(k):
        tile = (mine + k) % tiles
        if rows % 16 == 0:
            start = pl.multiple_of(tile * rows, 16)
            inner = product[pl.ds(start, rows), :]
        else:
            inner = jnp.concatenate(
                [product[pl.ds(tile * rows + i, 1), :] for i in range(rows)], axis=0
            )
        predicted[tile] = inner.astype(jnp.bfloat16)
        low = product[pl.ds(jnp.maximum(tile * rows - 1, 0), 1), :]
        high = product[pl.ds(jnp.minimum(tile * rows + rows, stations - 1), 1), :]
        low = jnp.where(tile == 0, 0.0, low)
        high = jnp.where(tile == tiles - 1, 0.0, high)
        pieces = [edge[:, i : i + 128] for edge in (low, high) for i in range(0, width, 128)]
        halo[tile] = jnp.concatenate(pieces, axis=0).astype(jnp.bfloat16)

        @pl.when(k < tiles)
        def _():
            tile_copy(*predicted_set, tile).start()
            tile_copy(*halo_set, tile).start()

    predicted_out[mine] = predicted[mine]
    halo_out[mine] = halo[mine]
    filtered_tables(weights_ref, shifted_ref, basis_out)

    @pl.loop(1, tiles)
    def _(k):
        for transfers in (recorded_set, predicted_set, halo_set):
            tile_arrival(*transfers, (mine + k) % tiles).wait_recv()

    @pl.loop(1, tiles)
    def _(k):
        for transfers in (recorded_set, predicted_set, halo_set):
            tile_copy(*transfers, (mine + k) % tiles).wait_send()

    for slot, peer in enumerate(peers):
        own_copy(slot, peer).wait_send()
        forward_copy(slot, peer).wait_send()
    own_copy(len(peers), sibling).wait_send()


def exchange(weights, shifted, real, imag, shard, tiles, lines):
    stations, width = shard.shape
    rows = stations // tiles
    vmem = pl.BlockSpec(memory_space=pltpu.VMEM)
    tile_shape = (tiles, rows, width)
    halo_shape = (tiles, 2 * width // 128, 128)
    sems = pltpu.SemaphoreType.DMA((tiles,))
    return pl.pallas_call(
        functools.partial(exchange_kernel, tiles, lines),
        out_shape=[
            jax.ShapeDtypeStruct(tile_shape, jnp.bfloat16),
            jax.ShapeDtypeStruct(tile_shape, jnp.bfloat16),
            jax.ShapeDtypeStruct(halo_shape, jnp.bfloat16),
            jax.ShapeDtypeStruct((rows, 3 * shifted.shape[1], shifted.shape[2]), jnp.bfloat16),
        ],
        in_specs=[pl.BlockSpec(memory_space=pltpu.SMEM)] + [vmem] * 5,
        out_specs=[vmem] * 4,
        scratch_shapes=[
            pltpu.VMEM((lines, stations, width), jnp.bfloat16),
            pltpu.VMEM((stations, width), jnp.float32),
            pltpu.VMEM(tile_shape, jnp.bfloat16),
            pltpu.VMEM(halo_shape, jnp.bfloat16),
        ]
        + [sems] * 6
        + [pltpu.SemaphoreType.DMA((lines,))] * 3,
        compiler_params=pltpu.CompilerParams(
            collective_id=0, has_side_effects=True, vmem_limit_bytes=40 * 1024 * 1024
        ),
        cost_estimate=pl.CostEstimate(
            flops=8 * lines * stations * stations * width // 2,
            bytes_accessed=2 * (lines + 5) * stations * width,
            transcendentals=0,
        ),
    )(weights, shifted, real, imag, shard, shard.reshape(tile_shape))


def body(operator, recorded, filter_coefficients, tap_delays):
    stations = operator.shape[1]
    tiles, lines = lax.axis_size("freq"), lax.axis_size("row")
    rows = stations // tiles
    shots = recorded.shape[3]
    table = inverse_lookup(tiles, NT).reshape(2 * tiles, NT)
    recorded_tiles, predicted_tiles, halo, basis = exchange(
        filter_coefficients,
        delayed_tables(tap_delays, table),
        operator[0, :, 0],
        operator[0, :, 1],
        recorded[0].reshape(stations, 2 * shots),
        tiles,
        lines,
    )
    halo = halo.reshape(tiles, 2, 2 * shots)

    def by_station(spectra):
        return jnp.swapaxes(spectra, 0, 1).reshape(spectra.shape[1], 2 * tiles, shots)

    return to_primaries(
        table,
        basis,
        by_station(recorded_tiles),
        by_station(jnp.concatenate([halo[:, :1], predicted_tiles, halo[:, 1:]], axis=1)),
    )


def solution(mesh):
    in_specs = (
        P("freq", "row", None, None),
        P("freq", "row", None, None),
        P(None, None, ("row", "freq")),
        P(),
    )
    out_specs = P(("row", "freq"), None, None)
    return jax.shard_map(body, mesh=mesh, in_specs=in_specs, out_specs=out_specs, check_vma=False)
```
